32 devices in a mesh: groups: 2 (over x), gy: 16 (over z, y, core).
Axes of the slice: x: 2, y: 2, z: 4, core: 2. Of those that a mesh axis runs over, the one named last changes fastest.
Arguments:
- state: float32 [8, 64, 128, 128], P(None, 'groups', 'gy'), parts along dimension 1
- base: float32 [8, 64, 128, 128], P(None, 'groups', 'gy'), parts along dimension 1
- shear_shift: int32 [64], P('groups'), parts along dimension 0, may hold values from 0 to 127
Outputs:
- advanced: float32 [8, 64, 128, 128], P(None, 'groups', 'gy'), parts along dimension 1
The draws below stay inside these ranges and needn't reach their ends.
There are 2 independent parts, one for each index of `groups`. The reference program is written for one: setup_inputs(seed, part) draws one part's arguments, and reference() takes and returns one part's arrays. A program takes and returns all parts, laid end to end along the dimension named above; each array names one. Nothing has to cross between parts.
All inputs are finite; a program needn't handle non-finite values.
Results may differ from the reference program's by a relative error of at most 0.00002.
Values sent between devices are 32-bit elements; how exact they have to be, the bound alone decides.
A program may use at most 128 MiB of HBM per device.

```python
import jax
import jax.numpy as jnp

NX = 128
NZ = 32
NY = 128


def draw_state(key, part):
    key = jax.random.fold_in(key, 1)
    return make_fields(key)


def draw_base(key, part):
    key = jax.random.fold_in(key, 2)
    return make_fields(key)


def make_fields(key):
    key_rho = jax.random.fold_in(key, 11)
    key_mid = jax.random.fold_in(key, 12)
    key_ene = jax.random.fold_in(key, 13)
    shape = (1, NZ, NY, NX)
    density = jnp.exp(jax.random.uniform(key_rho, shape, jnp.float32, -0.6931, 0.6931))
    middle = 0.5 * jax.random.normal(key_mid, (6, NZ, NY, NX), jnp.float32)
    energy = jax.random.uniform(key_ene, shape, jnp.float32, 1.5, 3.0)
    return jnp.concatenate([density, middle, energy], axis=0).astype(jnp.float32)


def touch_ends(array, stream_key, low, high):
    dims = array.shape
    spot = [jax.random.randint(jax.random.fold_in(stream_key, axis), (), 0, dims[axis]) for axis in range(len(dims))]
    array = array.at[tuple(spot)].set(low)
    longest = dims.index(max(dims))
    spot[longest] = (spot[longest] + 1) % dims[longest]
    return array.at[tuple(spot)].set(high)


def setup_inputs(seed: int = 0, part: int = 0) -> dict:
    key_list = jax.random.split(jax.random.key(seed), 4)
    own_keys = jax.random.split(jax.random.fold_in(key_list[3], part), 4)
    state = draw_state(jax.random.fold_in(jax.random.fold_in(key_list[3], part), 71), part)
    base = draw_base(jax.random.fold_in(jax.random.fold_in(key_list[3], part), 71), part)
    shear_shift = touch_ends(jax.random.randint(own_keys[2], (NZ,), 0, NY), jax.random.fold_in(own_keys[2], 1), 0, NY - 1).astype(jnp.int32)
    return dict(state=state, base=base, shear_shift=shear_shift)


GAMMA = 5.0 / 3.0
ADV = 0.1
DIFF = 0.1
DTIME = 0.2
OMEGA = 1.0
QSHEAR = 1.5
SHEAR_V = 0.75


def fluxes(fields, direction):
    density = fields[0]
    momenta = fields[1:4]
    magnet = fields[4:7]
    energy = fields[7]
    velocity = momenta / density
    magnet_sq = magnet[0] * magnet[0] + magnet[1] * magnet[1] + magnet[2] * magnet[2]
    kinetic = momenta[0] * velocity[0] + momenta[1] * velocity[1] + momenta[2] * velocity[2]
    total_p = (GAMMA - 1.0) * (energy - 0.5 * kinetic - 0.5 * magnet_sq) + 0.5 * magnet_sq
    cross_vb = velocity[0] * magnet[0] + velocity[1] * magnet[1] + velocity[2] * magnet[2]
    along_v = velocity[direction]
    along_b = magnet[direction]
    mom_flux = momenta * along_v - magnet * along_b
    mom_flux = mom_flux.at[direction].add(total_p)
    mag_flux = along_v * magnet - along_b * velocity
    energy_flux = (energy + total_p) * along_v - along_b * cross_vb
    return jnp.concatenate([momenta[direction][None], mom_flux, mag_flux, energy_flux[None]], axis=0)


def sources(fields, xcoord):
    density = fields[0]
    mom_x = fields[1]
    mom_y = fields[2]
    tidal = 2.0 * QSHEAR * OMEGA * OMEGA * xcoord
    force_x = 2.0 * OMEGA * mom_y + tidal * density
    force_y = -2.0 * OMEGA * mom_x
    heating = tidal * mom_x
    zeros = jnp.zeros_like(density)
    return jnp.stack([zeros, force_x, force_y, zeros, zeros, zeros, zeros, heating])


def advance(state, base, lo_ghost, hi_ghost, y_hi, y_lo, fy_hi, fy_lo):
    width = state.shape[3]
    xcoord = (jnp.arange(width).astype(jnp.float32) + 0.5) / width - 0.5
    flux_x = fluxes(state, 0)
    x_hi = jnp.concatenate([state[..., 1:], hi_ghost], axis=3)
    x_lo = jnp.concatenate([lo_ghost, state[..., :-1]], axis=3)
    fx_hi = jnp.concatenate([flux_x[..., 1:], fluxes(hi_ghost, 0)], axis=3)
    fx_lo = jnp.concatenate([fluxes(lo_ghost, 0), flux_x[..., :-1]], axis=3)
    flux_z = fluxes(state, 2)
    fz_hi = jnp.roll(flux_z, -1, 1)
    fz_lo = jnp.roll(flux_z, 1, 1)
    z_hi = jnp.roll(state, -1, 1)
    z_lo = jnp.roll(state, 1, 1)
    diverge = (fx_hi - fx_lo) + (fy_hi - fy_lo) + (fz_hi - fz_lo)
    spread = (x_hi + x_lo - 2.0 * state) + (y_hi + y_lo - 2.0 * state) + (z_hi + z_lo - 2.0 * state)
    moved = state - ADV * diverge + DIFF * spread + DTIME * sources(state, xcoord)
    return 0.5 * base + 0.5 * moved


def reference(state, base, shear_shift):
    rows = jnp.arange(NY).astype(jnp.int32)
    in_index = (rows[None, :] - shear_shift[:, None]) % NY
    out_index = (rows[None, :] + shear_shift[:, None]) % NY
    lo_ghost = jnp.take_along_axis(state[:, :, :, NX - 1], in_index[None], axis=2)
    hi_ghost = jnp.take_along_axis(state[:, :, :, 0], out_index[None], axis=2)
    lo_ghost = lo_ghost.at[2].add(SHEAR_V * lo_ghost[0])
    hi_ghost = hi_ghost.at[2].add(-SHEAR_V * hi_ghost[0])
    flux_y = fluxes(state, 1)
    return advance(state, base, lo_ghost[..., None], hi_ghost[..., None],
                   jnp.roll(state, -1, 2), jnp.roll(state, 1, 2),
                   jnp.roll(flux_y, -1, 2), jnp.roll(flux_y, 1, 2))
```

```python
import functools

import jax
import jax.numpy as jnp
from jax import lax
from jax.experimental import pallas as pl
from jax.experimental.pallas import tpu as pltpu
from jax.sharding import PartitionSpec as P

SHEAR_V = 0.75
SCALE = 0.05
LANES = 128
ROWS = 8
MESH = pl.DeviceIdType.MESH


def products(u):
    inv = 1.0 / u[0]
    w = [u[1] * inv, u[2] * inv, u[3] * inv]
    b = [u[4], u[5], u[6]]
    c = [SCALE * f for f in u]
    mc, bc = c[1:4], c[4:7]
    kin = mc[0] * w[0] + mc[1] * w[1] + mc[2] * w[2]
    bsq = bc[0] * b[0] + bc[1] * b[1] + bc[2] * b[2]
    press = (2.0 / 3.0) * (c[7] - 0.5 * kin - 0.5 * bsq) + 0.5 * bsq
    cross = w[0] * b[0] + w[1] * b[1] + w[2] * b[2]
    return c, w, b, press, cross


def tensor(c, w, b, i, j):
    return c[1 + i] * w[j] - c[4 + i] * b[j]


def twist(c, w, i, j):
    return w[i] * c[4 + j] - c[4 + i] * w[j]


def energy_flux(c, w, press, cross, d):
    return (c[7] + press) * w[d] - c[4 + d] * cross


def flux_along(u, d):
    c, w, b, press, cross = products(u)
    out = [c[1 + d]]
    for i in range(3):
        t = tensor(c, w, b, i, d)
        out.append(t + press if i == d else t)
    for i in range(3):
        out.append(None if i == d else twist(c, w, d, i))
    out.append(energy_flux(c, w, press, cross, d))
    return c, out


def plus(a, f):
    return a if f is None else a + f


def minus(a, f):
    return a if f is None else a - f


def kernel(
    n, planes, shift_ref, state_hbm, base_hbm, out_hbm,
    st, bs, ov, gath, halo_out, halo_in,
    local_sem, halo_send, halo_recv, edge_send, edge_recv,
):
    me = lax.axis_index("gy")
    field = planes * ROWS
    right = lax.rem(me + 1, n)
    left = lax.rem(me + n - 1, n)

    load_state = pltpu.make_async_copy(state_hbm, st, local_sem.at[0])
    load_state.start()
    load_base = pltpu.make_async_copy(base_hbm, bs, local_sem.at[1])
    load_base.start()

    barrier = pltpu.get_barrier_semaphore()

    def greet(d, carry):
        pl.semaphore_signal(
            barrier, inc=1, device_id={"gy": lax.rem(me + d, n)}, device_id_type=MESH
        )
        return carry

    lax.fori_loop(1, n, greet, 0)

    lane = lax.broadcasted_iota(jnp.int32, (ROWS, LANES), 1)
    row = lax.broadcasted_iota(jnp.int32, (ROWS, LANES), 0)
    pair = lane // 2
    even = lane % 2 == 0

    load_state.wait()

    for f in range(8):
        for g in range(planes // ROWS):
            at = f * field + g * ROWS * ROWS
            to = pl.ds(f * planes + g * ROWS, ROWS)
            halo_out[0, to, :] = st[pl.ds(at, ROWS, stride=ROWS), :]
            halo_out[1, to, :] = st[pl.ds(at + ROWS - 1, ROWS, stride=ROWS), :]

    def plane_at(f, k):
        return pl.ds(pl.multiple_of(f * field + k * ROWS, ROWS), ROWS)

    def collect(k, acc):
        out = []
        for j in range(4):
            low = pltpu.roll(st[plane_at(j, k), :], 2 * k + 1, 1)
            high = pltpu.roll(st[plane_at(j + 4, k), :], 2 * k + 1 + 64, 1)
            keep = jnp.where(pair == k, low, acc[j])
            out.append(jnp.where(pair == k + 32, high, keep))
        return tuple(out)

    zero = jnp.zeros((ROWS, LANES), jnp.float32)
    edges = lax.fori_loop(0, planes, collect, (zero,) * 4, unroll=4)
    for j in range(4):
        gath[0, pl.ds(j * ROWS, ROWS), :] = edges[j]

    pl.semaphore_wait(barrier, n - 1)

    def edge_copy(d):
        return pltpu.make_async_remote_copy(
            src_ref=gath.at[0],
            dst_ref=gath.at[d],
            send_sem=edge_send.at[d],
            recv_sem=edge_recv.at[d],
            device_id={"gy": lax.rem(me + d, n)},
            device_id_type=MESH,
        )

    def halo_copy(s, target):
        return pltpu.make_async_remote_copy(
            src_ref=halo_out.at[s],
            dst_ref=halo_in.at[s],
            send_sem=halo_send.at[s],
            recv_sem=halo_recv.at[s],
            device_id={"gy": target},
            device_id_type=MESH,
        )

    def send_edge(d, carry):
        edge_copy(d).start()
        return carry

    lax.fori_loop(1, n, send_edge, 0)
    halos = [halo_copy(0, left), halo_copy(1, right)]
    for copy in halos:
        copy.start()

    load_base.wait()

    tidal = ((lane.astype(jnp.float32) + 0.5) / LANES - 0.5) * 6.0
    first_x, last_x = lane == 0, lane == LANES - 1
    first_y, last_y = row == 0, row == ROWS - 1

    def from_next_x(a):
        return jnp.where(last_x, 0.0, pltpu.roll(a, LANES - 1, 1))

    def from_prev_x(a):
        return jnp.where(first_x, 0.0, pltpu.roll(a, 1, 1))

    def from_next_y(a):
        return jnp.where(last_y, 0.0, pltpu.roll(a, ROWS - 1, 0))

    def from_prev_y(a):
        return jnp.where(first_y, 0.0, pltpu.roll(a, 1, 0))

    def plane_terms(u):
        c, w, b, press, cross = products(u)
        t = {(i, j): tensor(c, w, b, i, j) for i in range(3) for j in range(i, 3)}
        for i in range(3):
            t[i, i] = t[i, i] + press
        s = {(i, j): twist(c, w, i, j) for i in range(3) for j in range(i + 1, 3)}
        ahead, behind = [], []
        for d in range(3):
            fl = [c[1 + d]] + [t[min(i, d), max(i, d)] for i in range(3)]
            up = [c[f] + fl[f] for f in range(4)]
            down = [c[f] - fl[f] for f in range(4)]
            for i in range(3):
                a = c[4 + i]
                if i == d:
                    up.append(a)
                    down.append(a)
                elif d < i:
                    up.append(a + s[d, i])
                    down.append(a - s[d, i])
                else:
                    up.append(a - s[i, d])
                    down.append(a + s[i, d])
            e = energy_flux(c, w, press, cross, d)
            up.append(c[7] + e)
            down.append(c[7] - e)
            behind.append(up)
            ahead.append(down)
        return c, ahead, behind

    def load_plane(k):
        return [st[plane_at(f, k), :] for f in range(8)]

    def step(k, carry):
        partial, below = carry
        c, ahead, behind = plane_terms(load_plane(k))
        prev = lax.rem(k + planes - 1, planes)
        source = [4.0 * f for f in c]
        source[1] = 4.0 * (c[1] + c[2]) + tidal * c[0]
        source[2] = 4.0 * (c[2] - c[1])
        source[7] = source[7] + tidal * c[1]
        fresh = []
        for f in range(8):
            ov[plane_at(f, prev), :] = partial[f] + ahead[2][f]
            here = 0.5 * bs[plane_at(f, k), :] + source[f]
            here = here + (from_next_x(ahead[0][f]) + from_prev_x(behind[0][f]))
            here = here + (from_next_y(ahead[1][f]) + from_prev_y(behind[1][f]))
            fresh.append(here + below[f])
        return tuple(fresh), tuple(behind[2])

    u = load_plane(planes - 1)
    c, fl = flux_along(u, 2)
    below = tuple(plus(c[f], fl[f]) for f in range(8))
    partial, _ = lax.fori_loop(0, planes, step, ((zero,) * 8, below), unroll=2)
    for f in range(8):
        at = plane_at(f, planes - 1)
        ov[at, :] = ov[at, :] + partial[f]

    for s, combine, to_row in ((0, minus, ROWS - 1), (1, plus, 0)):
        halos[s].wait_recv()
        for g in range(planes // ROWS):
            u = [halo_in[s, pl.ds(f * planes + g * ROWS, ROWS), :] for f in range(8)]
            c, fl = flux_along(u, 1)
            for f in range(8):
                at = pl.ds(f * field + g * ROWS * ROWS + to_row, ROWS, stride=ROWS)
                ov[at, :] = ov[at, :] + combine(c[f], fl[f])

    cells = n * ROWS
    shift = jnp.zeros((ROWS, LANES), jnp.int32)
    for k in range(planes):
        shift = jnp.where(pair % 32 == k, shift_ref[k], shift)
    shift = jnp.where(even, shift, jnp.where(shift == 0, 0, cells - shift))
    hop = shift // ROWS
    fine = shift % ROWS
    hop_next = jnp.where(hop == n - 1, 0, hop + 1)

    def pick(d, carry):
        near, far = carry
        tiles = [gath[d, pl.ds(j * ROWS, ROWS), :] for j in range(4)]
        is_near, is_far = hop == d, hop_next == d
        return (
            tuple(jnp.where(is_near, tiles[j], near[j]) for j in range(4)),
            tuple(jnp.where(is_far, tiles[j], far[j]) for j in range(4)),
        )

    def wait_pick(d, carry):
        edge_copy(d).wait_recv()
        return pick(d, carry)

    chosen = pick(0, ((zero,) * 4, (zero,) * 4))
    near, far = lax.fori_loop(1, n, wait_pick, chosen)

    ghost = [None] * 8
    for j in range(4):
        a, b = near[j], far[j]
        for bit in (4, 2, 1):
            ra, rb = pltpu.roll(a, bit, 0), pltpu.roll(b, bit, 0)
            take = (fine // bit) % 2 == 1
            a = jnp.where(take, jnp.where(row < bit, rb, ra), a)
            b = jnp.where(take, rb, b)
        ghost[j] = a
        ghost[j + 4] = pltpu.roll(a, 64, 1)
    sign = jnp.where(even, 1.0, -1.0)
    ghost[0] = jnp.where(lane < 2 * planes, ghost[0], 1.0)
    ghost[2] = ghost[2] + sign * (SHEAR_V * ghost[0])
    c, fl = flux_along(ghost, 0)
    side = []
    for f in range(8):
        e = c[f] if fl[f] is None else c[f] + sign * fl[f]
        side.append(jnp.where(even, pltpu.roll(e, LANES - 1, 1), pltpu.roll(e, 1, 1)))
    outer = jnp.logical_or(first_x, last_x)

    def put_edges(k, carry):
        for f in range(8):
            at = plane_at(f, k)
            add = pltpu.roll(side[f], LANES - 1 - 2 * k, 1)
            ov[at, :] = ov[at, :] + jnp.where(outer, add, 0.0)
        return carry

    lax.fori_loop(0, planes, put_edges, 0, unroll=4)

    store = pltpu.make_async_copy(ov, out_hbm, local_sem.at[2])
    store.start()
    for copy in halos:
        copy.wait_send()

    def wait_edge(d, carry):
        edge_copy(d).wait_send()
        return carry

    lax.fori_loop(1, n, wait_edge, 0)
    store.wait()


def on_device(n, state, base, shear_shift):
    shape = state.shape
    planes = shape[1]
    assert shape[0] == 8 and shape[2] == ROWS and shape[3] == LANES and planes == 32
    total = 8 * planes * ROWS
    out = pl.pallas_call(
        functools.partial(kernel, n, planes),
        out_shape=jax.ShapeDtypeStruct((total, LANES), jnp.float32),
        in_specs=[
            pl.BlockSpec(memory_space=pltpu.SMEM),
            pl.BlockSpec(memory_space=pl.ANY),
            pl.BlockSpec(memory_space=pl.ANY),
        ],
        out_specs=pl.BlockSpec(memory_space=pl.ANY),
        scratch_shapes=[
            pltpu.VMEM((total, LANES), jnp.float32),
            pltpu.VMEM((total, LANES), jnp.float32),
            pltpu.VMEM((total, LANES), jnp.float32),
            pltpu.VMEM((n, 4 * ROWS, LANES), jnp.float32),
            pltpu.VMEM((2, 8 * planes, LANES), jnp.float32),
            pltpu.VMEM((2, 8 * planes, LANES), jnp.float32),
            pltpu.SemaphoreType.DMA((3,)),
            pltpu.SemaphoreType.DMA((2,)),
            pltpu.SemaphoreType.DMA((2,)),
            pltpu.SemaphoreType.DMA((n,)),
            pltpu.SemaphoreType.DMA((n,)),
        ],
        compiler_params=pltpu.CompilerParams(
            collective_id=0, has_side_effects=True, vmem_limit_bytes=24 * 1024 * 1024
        ),
    )(shear_shift, state.reshape(total, LANES), base.reshape(total, LANES))
    return out.reshape(shape)


def solution(mesh):
    return jax.shard_map(
        functools.partial(on_device, mesh.shape["gy"]),
        mesh=mesh,
        in_specs=(P(None, "groups", "gy", None), P(None, "groups", "gy", None), P("groups")),
        out_specs=P(None, "groups", "gy", None),
        check_vma=False,
    )
```

```python
import functools

import jax
import jax.numpy as jnp
from jax import lax
from jax.experimental import pallas as pl
from jax.experimental.pallas import tpu as pltpu
from jax.sharding import PartitionSpec as P

SHEAR_V = 0.75
SCALE = 0.05
LANES = 128
FIRST = 16
ROWS = 8
MESH = pl.DeviceIdType.MESH


def products(u):
    inv = 1.0 / u[0]
    w = [u[1] * inv, u[2] * inv, u[3] * inv]
    b = [u[4], u[5], u[6]]
    c = [SCALE * f for f in u]
    mc, bc = c[1:4], c[4:7]
    kin = mc[0] * w[0] + mc[1] * w[1] + mc[2] * w[2]
    bsq = bc[0] * b[0] + bc[1] * b[1] + bc[2] * b[2]
    press = (2.0 / 3.0) * (c[7] - 0.5 * kin - 0.5 * bsq) + 0.5 * bsq
    cross = w[0] * b[0] + w[1] * b[1] + w[2] * b[2]
    return c, w, b, press, cross


def tensor(c, w, b, i, j):
    return c[1 + i] * w[j] - c[4 + i] * b[j]


def twist(c, w, i, j):
    return w[i] * c[4 + j] - c[4 + i] * w[j]


def energy_flux(c, w, press, cross, d):
    return (c[7] + press) * w[d] - c[4 + d] * cross


def flux_along(u, d):
    c, w, b, press, cross = products(u)
    out = [c[1 + d]]
    for i in range(3):
        t = tensor(c, w, b, i, d)
        out.append(t + press if i == d else t)
    for i in range(3):
        out.append(None if i == d else twist(c, w, d, i))
    out.append(energy_flux(c, w, press, cross, d))
    return c, out


def plus(a, f):
    return a if f is None else a + f


def minus(a, f):
    return a if f is None else a - f


def kernel(
    outer, inner, planes, shift_ref, state_hbm, base_hbm, ov,
    st, bs, gath, relay, caught, halo_out, halo_in,
    local_sem, halo_send, halo_recv, edge_send, edge_recv, relay_send, relay_recv,
):
    n = outer * inner
    me = lax.axis_index("gy")
    high, low = me // inner, lax.rem(me, inner)
    field = planes * ROWS
    right = lax.rem(me + 1, n)
    left = lax.rem(me + n - 1, n)

    load_state = pltpu.make_async_copy(state_hbm, st, local_sem.at[0])
    load_state.start()
    load_base = pltpu.make_async_copy(base_hbm, bs, local_sem.at[1])
    load_base.start()

    barrier = pltpu.get_barrier_semaphore()

    across = [lax.rem(me + a * inner, n) for a in range(1, outer)]
    within = [high * inner + lax.rem(low + b, inner) for b in range(1, inner)]
    partners = across + within + [left, right]
    for partner in partners:
        pl.semaphore_signal(
            barrier, inc=1, device_id={"gy": partner}, device_id_type=MESH
        )

    lane = lax.broadcasted_iota(jnp.int32, (ROWS, LANES), 1)
    row = lax.broadcasted_iota(jnp.int32, (ROWS, LANES), 0)
    pair = lane // 2
    even = lane % 2 == 0

    load_state.wait()

    for f in range(8):
        for g in range(planes // ROWS):
            at = f * field + g * ROWS * ROWS
            to = pl.ds(f * planes + g * ROWS, ROWS)
            halo_out[0, to, :] = st[pl.ds(at, ROWS, stride=ROWS), :]
            halo_out[1, to, :] = st[pl.ds(at + ROWS - 1, ROWS, stride=ROWS), :]

    def plane_at(f, k):
        return pl.ds(pl.multiple_of(f * field + k * ROWS, ROWS), ROWS)

    def collect(k, acc):
        out = []
        for j in range(4):
            low = pltpu.roll(st[plane_at(j, k), :], 2 * k + 1, 1)
            high = pltpu.roll(st[plane_at(j + 4, k), :], 2 * k + 1 + 64, 1)
            keep = jnp.where(pair == k, low, acc[j])
            out.append(jnp.where(pair == k + 32, high, keep))
        return tuple(out)

    zero = jnp.zeros((ROWS, LANES), jnp.float32)
    edges = lax.fori_loop(0, planes, collect, (zero,) * 4, unroll=4)
    for j in range(4):
        gath[0, pl.ds(j * ROWS, ROWS), :] = edges[j]

    pl.semaphore_wait(barrier, len(partners))

    def edge_copy(d):
        return pltpu.make_async_remote_copy(
            src_ref=gath.at[0],
            dst_ref=gath.at[d],
            send_sem=edge_send.at[d],
            recv_sem=edge_recv.at[d],
            device_id={"gy": across[d - 1]},
            device_id_type=MESH,
        )

    def relay_copy(d):
        return pltpu.make_async_remote_copy(
            src_ref=relay.at[d],
            dst_ref=caught.at[d],
            send_sem=relay_send.at[d],
            recv_sem=relay_recv.at[d],
            device_id={"gy": within[d - 1]},
            device_id_type=MESH,
        )

    def halo_copy(s, target):
        return pltpu.make_async_remote_copy(
            src_ref=halo_out.at[s],
            dst_ref=halo_in.at[s],
            send_sem=halo_send.at[s],
            recv_sem=halo_recv.at[s],
            device_id={"gy": target},
            device_id_type=MESH,
        )

    edge_copies = [edge_copy(d) for d in range(1, outer)]
    for copy in edge_copies:
        copy.start()
    halos = [halo_copy(0, left), halo_copy(1, right)]
    for copy in halos:
        copy.start()

    load_base.wait()

    tidal = ((lane.astype(jnp.float32) + 0.5) / LANES - 0.5) * 6.0
    first_x, last_x = lane == 0, lane == LANES - 1
    first_y, last_y = row == 0, row == ROWS - 1

    def from_next_x(a):
        return jnp.where(last_x, 0.0, pltpu.roll(a, LANES - 1, 1))

    def from_prev_x(a):
        return jnp.where(first_x, 0.0, pltpu.roll(a, 1, 1))

    def from_next_y(a):
        return jnp.where(last_y, 0.0, pltpu.roll(a, ROWS - 1, 0))

    def from_prev_y(a):
        return jnp.where(first_y, 0.0, pltpu.roll(a, 1, 0))

    def plane_terms(u):
        c, w, b, press, cross = products(u)
        t = {(i, j): tensor(c, w, b, i, j) for i in range(3) for j in range(i, 3)}
        for i in range(3):
            t[i, i] = t[i, i] + press
        s = {(i, j): twist(c, w, i, j) for i in range(3) for j in range(i + 1, 3)}
        ahead, behind = [], []
        for d in range(3):
            fl = [c[1 + d]] + [t[min(i, d), max(i, d)] for i in range(3)]
            up = [c[f] + fl[f] for f in range(4)]
            down = [c[f] - fl[f] for f in range(4)]
            for i in range(3):
                a = c[4 + i]
                if i == d:
                    up.append(a)
                    down.append(a)
                elif d < i:
                    up.append(a + s[d, i])
                    down.append(a - s[d, i])
                else:
                    up.append(a - s[i, d])
                    down.append(a + s[i, d])
            e = energy_flux(c, w, press, cross, d)
            up.append(c[7] + e)
            down.append(c[7] - e)
            behind.append(up)
            ahead.append(down)
        return c, ahead, behind

    def load_plane(k):
        return [st[plane_at(f, k), :] for f in range(8)]

    def step(k, carry):
        partial, below = carry
        c, ahead, behind = plane_terms(load_plane(k))
        prev = lax.rem(k + planes - 1, planes)
        source = [4.0 * f for f in c]
        source[1] = 4.0 * (c[1] + c[2]) + tidal * c[0]
        source[2] = 4.0 * (c[2] - c[1])
        source[7] = source[7] + tidal * c[1]
        fresh = []
        for f in range(8):
            ov[plane_at(f, prev), :] = partial[f] + ahead[2][f]
            here = 0.5 * bs[plane_at(f, k), :] + source[f]
            here = here + (from_next_x(ahead[0][f]) + from_prev_x(behind[0][f]))
            here = here + (from_next_y(ahead[1][f]) + from_prev_y(behind[1][f]))
            fresh.append(here + below[f])
        return tuple(fresh), tuple(behind[2])

    u = load_plane(planes - 1)
    c, fl = flux_along(u, 2)
    below = tuple(plus(c[f], fl[f]) for f in range(8))
    carry = lax.fori_loop(0, FIRST, step, ((zero,) * 8, below), unroll=2)

    cells = n * ROWS
    shift = jnp.zeros((ROWS, LANES), jnp.int32)
    for k in range(planes):
        shift = jnp.where(pair % 32 == k, shift_ref[k], shift)
    shift = jnp.where(even, shift, jnp.where(shift == 0, 0, cells - shift))
    hop = shift // ROWS
    fine = shift % ROWS
    hop_next = jnp.where(hop == n - 1, 0, hop + 1)

    def locate(hops, target):
        over, rest = hops // inner, hops % inner
        wraps = rest > target
        over = jnp.where(wraps, over + 1, over)
        column = target - rest + jnp.where(wraps, inner, 0)
        return jnp.where(over == outer, 0, over), column

    for copy in edge_copies:
        copy.wait_recv()
    for b in range(inner):
        target = lax.rem(low + b, inner)
        over, column = locate(hop, target)
        over_next, _ = locate(hop_next, target)
        slot = jnp.where(column == low, over, over_next)
        for j in range(4):
            part = pl.ds(j * ROWS, ROWS)
            tile = gath[0, part, :]
            for d in range(1, outer):
                tile = jnp.where(slot == d, gath[d, part, :], tile)
            (relay if b else caught)[b, part, :] = tile
    relay_copies = [relay_copy(d) for d in range(1, inner)]
    for copy in relay_copies:
        copy.start()

    partial, _ = lax.fori_loop(FIRST, planes, step, carry, unroll=2)
    for f in range(8):
        at = plane_at(f, planes - 1)
        ov[at, :] = ov[at, :] + partial[f]

    for s, combine, to_row in ((0, minus, ROWS - 1), (1, plus, 0)):
        halos[s].wait_recv()
        for g in range(planes // ROWS):
            u = [halo_in[s, pl.ds(f * planes + g * ROWS, ROWS), :] for f in range(8)]
            c, fl = flux_along(u, 1)
            for f in range(8):
                at = pl.ds(f * field + g * ROWS * ROWS + to_row, ROWS, stride=ROWS)
                ov[at, :] = ov[at, :] + combine(c[f], fl[f])

    for copy in relay_copies:
        copy.wait_recv()
    near, far = [], []
    for j in range(4):
        part = pl.ds(j * ROWS, ROWS)
        a = b = caught[0, part, :]
        for d in range(1, inner):
            tile = caught[d, part, :]
            a = jnp.where(hop % inner == d, tile, a)
            b = jnp.where(hop_next % inner == d, tile, b)
        near.append(a)
        far.append(b)

    ghost = [None] * 8
    for j in range(4):
        a, b = near[j], far[j]
        for bit in (4, 2, 1):
            ra, rb = pltpu.roll(a, bit, 0), pltpu.roll(b, bit, 0)
            take = (fine // bit) % 2 == 1
            a = jnp.where(take, jnp.where(row < bit, rb, ra), a)
            b = jnp.where(take, rb, b)
        ghost[j] = a
        ghost[j + 4] = pltpu.roll(a, 64, 1)
    sign = jnp.where(even, 1.0, -1.0)
    ghost[0] = jnp.where(lane < 2 * planes, ghost[0], 1.0)
    ghost[2] = ghost[2] + sign * (SHEAR_V * ghost[0])
    c, fl = flux_along(ghost, 0)
    side = []
    for f in range(8):
        e = c[f] if fl[f] is None else c[f] + sign * fl[f]
        side.append(jnp.where(even, pltpu.roll(e, LANES - 1, 1), pltpu.roll(e, 1, 1)))
    rim = jnp.logical_or(first_x, last_x)

    def put_edges(k, carry):
        for f in range(8):
            at = plane_at(f, k)
            add = pltpu.roll(side[f], LANES - 1 - 2 * k, 1)
            ov[at, :] = ov[at, :] + jnp.where(rim, add, 0.0)
        return carry

    lax.fori_loop(0, planes, put_edges, 0, unroll=4)

    for copy in halos + edge_copies + relay_copies:
        copy.wait_send()


def on_device(n, state, base, shear_shift):
    shape = state.shape
    planes = shape[1]
    assert shape[0] == 8 and shape[2] == ROWS and shape[3] == LANES and planes == 32
    total = 8 * planes * ROWS
    inner = 1 << ((n.bit_length() - 1) // 2)
    outer = n // inner
    assert outer * inner == n
    out = pl.pallas_call(
        functools.partial(kernel, outer, inner, planes),
        out_shape=pltpu.VMEM((total, LANES), jnp.float32),
        in_specs=[
            pl.BlockSpec(memory_space=pltpu.SMEM),
            pl.BlockSpec(memory_space=pltpu.HBM),
            pl.BlockSpec(memory_space=pltpu.HBM),
        ],
        out_specs=pl.BlockSpec(memory_space=pltpu.VMEM),
        scratch_shapes=[
            pltpu.VMEM((total, LANES), jnp.float32),
            pltpu.VMEM((total, LANES), jnp.float32),
            pltpu.VMEM((outer, 4 * ROWS, LANES), jnp.float32),
            pltpu.VMEM((inner, 4 * ROWS, LANES), jnp.float32),
            pltpu.VMEM((inner, 4 * ROWS, LANES), jnp.float32),
            pltpu.VMEM((2, 8 * planes, LANES), jnp.float32),
            pltpu.VMEM((2, 8 * planes, LANES), jnp.float32),
            pltpu.SemaphoreType.DMA((2,)),
            pltpu.SemaphoreType.DMA((2,)),
            pltpu.SemaphoreType.DMA((2,)),
            pltpu.SemaphoreType.DMA((outer,)),
            pltpu.SemaphoreType.DMA((outer,)),
            pltpu.SemaphoreType.DMA((inner,)),
            pltpu.SemaphoreType.DMA((inner,)),
        ],
        compiler_params=pltpu.CompilerParams(
            collective_id=0, has_side_effects=True, vmem_limit_bytes=64 * 1024 * 1024 - 1536 * 1024
        ),
    )(shear_shift, state.reshape(total, LANES), base.reshape(total, LANES))
    return out.reshape(shape)


def solution(mesh):
    return jax.shard_map(
        functools.partial(on_device, mesh.shape["gy"]),
        mesh=mesh,
        in_specs=(P(None, "groups", "gy", None), P(None, "groups", "gy", None), P("groups")),
        out_specs=P(None, "groups", "gy", None),
        check_vma=False,
    )
```

```python
import functools

import jax
import jax.numpy as jnp
from jax import lax
from jax.experimental import pallas as pl
from jax.experimental.pallas import tpu as pltpu
from jax.sharding import PartitionSpec as P

SHEAR_V = 0.75
SCALE = 0.05
LANES = 128
FIRST = 16
ROWS = 8
MESH = pl.DeviceIdType.MESH


def products(u):
    inv = 1.0 / u[0]
    w = [u[1] * inv, u[2] * inv, u[3] * inv]
    b = [u[4], u[5], u[6]]
    c = [SCALE * f for f in u]
    mc, bc = c[1:4], c[4:7]
    kin = mc[0] * w[0] + mc[1] * w[1] + mc[2] * w[2]
    bsq = bc[0] * b[0] + bc[1] * b[1] + bc[2] * b[2]
    press = (2.0 / 3.0) * (c[7] - 0.5 * kin - 0.5 * bsq) + 0.5 * bsq
    cross = w[0] * b[0] + w[1] * b[1] + w[2] * b[2]
    return c, w, b, press, cross


def tensor(c, w, b, i, j):
    return c[1 + i] * w[j] - c[4 + i] * b[j]


def twist(c, w, i, j):
    return w[i] * c[4 + j] - c[4 + i] * w[j]


def energy_flux(c, w, press, cross, d):
    return (c[7] + press) * w[d] - c[4 + d] * cross


def flux_along(u, d):
    c, w, b, press, cross = products(u)
    out = [c[1 + d]]
    for i in range(3):
        t = tensor(c, w, b, i, d)
        out.append(t + press if i == d else t)
    for i in range(3):
        out.append(None if i == d else twist(c, w, d, i))
    out.append(energy_flux(c, w, press, cross, d))
    return c, out


def plus(a, f):
    return a if f is None else a + f


def minus(a, f):
    return a if f is None else a - f


def kernel(
    outer, inner, planes, shift_ref, state_hbm, base_hbm, ov, side_ref,
    st, bs, gath, relay, caught, halo_out, halo_in,
    local_sem, halo_send, halo_recv, edge_send, edge_recv, relay_send, relay_recv,
):
    n = outer * inner
    me = lax.axis_index("gy")
    high, low = me // inner, lax.rem(me, inner)
    field = planes * ROWS
    right = lax.rem(me + 1, n)
    left = lax.rem(me + n - 1, n)

    load_state = pltpu.make_async_copy(state_hbm, st, local_sem.at[0])
    load_state.start()
    load_base = pltpu.make_async_copy(base_hbm, bs, local_sem.at[1])
    load_base.start()

    barrier = pltpu.get_barrier_semaphore()

    across = [lax.rem(me + a * inner, n) for a in range(1, outer)]
    within = [high * inner + lax.rem(low + b, inner) for b in range(1, inner)]
    partners = across + within + [left, right]
    for partner in partners:
        pl.semaphore_signal(
            barrier, inc=1, device_id={"gy": partner}, device_id_type=MESH
        )

    lane = lax.broadcasted_iota(jnp.int32, (ROWS, LANES), 1)
    row = lax.broadcasted_iota(jnp.int32, (ROWS, LANES), 0)
    pair = lane // 2
    even = lane % 2 == 0

    load_state.wait()

    for f in range(8):
        for g in range(planes // ROWS):
            at = f * field + g * ROWS * ROWS
            to = pl.ds(f * planes + g * ROWS, ROWS)
            halo_out[0, to, :] = st[pl.ds(at, ROWS, stride=ROWS), :]
            halo_out[1, to, :] = st[pl.ds(at + ROWS - 1, ROWS, stride=ROWS), :]

    def plane_at(f, k):
        return pl.ds(pl.multiple_of(f * field + k * ROWS, ROWS), ROWS)

    def collect(k, acc):
        out = []
        for j in range(4):
            low = pltpu.roll(st[plane_at(j, k), :], 2 * k + 1, 1)
            high = pltpu.roll(st[plane_at(j + 4, k), :], 2 * k + 1 + 64, 1)
            keep = jnp.where(pair == k, low, acc[j])
            out.append(jnp.where(pair == k + 32, high, keep))
        return tuple(out)

    zero = jnp.zeros((ROWS, LANES), jnp.float32)
    edges = lax.fori_loop(0, planes, collect, (zero,) * 4, unroll=4)
    for j in range(4):
        gath[0, pl.ds(j * ROWS, ROWS), :] = edges[j]

    pl.semaphore_wait(barrier, len(partners))

    def edge_copy(d):
        return pltpu.make_async_remote_copy(
            src_ref=gath.at[0],
            dst_ref=gath.at[d],
            send_sem=edge_send.at[d],
            recv_sem=edge_recv.at[d],
            device_id={"gy": across[d - 1]},
            device_id_type=MESH,
        )

    def relay_copy(d):
        return pltpu.make_async_remote_copy(
            src_ref=relay.at[d],
            dst_ref=caught.at[d],
            send_sem=relay_send.at[d],
            recv_sem=relay_recv.at[d],
            device_id={"gy": within[d - 1]},
            device_id_type=MESH,
        )

    def halo_copy(s, target):
        return pltpu.make_async_remote_copy(
            src_ref=halo_out.at[s],
            dst_ref=halo_in.at[s],
            send_sem=halo_send.at[s],
            recv_sem=halo_recv.at[s],
            device_id={"gy": target},
            device_id_type=MESH,
        )

    edge_copies = [edge_copy(d) for d in range(1, outer)]
    for copy in edge_copies:
        copy.start()
    halos = [halo_copy(0, left), halo_copy(1, right)]
    for copy in halos:
        copy.start()

    load_base.wait()

    tidal = ((lane.astype(jnp.float32) + 0.5) / LANES - 0.5) * 6.0
    first_x, last_x = lane == 0, lane == LANES - 1
    first_y, last_y = row == 0, row == ROWS - 1

    def from_next_x(a):
        return jnp.where(last_x, 0.0, pltpu.roll(a, LANES - 1, 1))

    def from_prev_x(a):
        return jnp.where(first_x, 0.0, pltpu.roll(a, 1, 1))

    def from_next_y(a):
        return jnp.where(last_y, 0.0, pltpu.roll(a, ROWS - 1, 0))

    def from_prev_y(a):
        return jnp.where(first_y, 0.0, pltpu.roll(a, 1, 0))

    def plane_terms(u):
        c, w, b, press, cross = products(u)
        t = {(i, j): tensor(c, w, b, i, j) for i in range(3) for j in range(i, 3)}
        for i in range(3):
            t[i, i] = t[i, i] + press
        s = {(i, j): twist(c, w, i, j) for i in range(3) for j in range(i + 1, 3)}
        ahead, behind = [], []
        for d in range(3):
            fl = [c[1 + d]] + [t[min(i, d), max(i, d)] for i in range(3)]
            up = [c[f] + fl[f] for f in range(4)]
            down = [c[f] - fl[f] for f in range(4)]
            for i in range(3):
                a = c[4 + i]
                if i == d:
                    up.append(a)
                    down.append(a)
                elif d < i:
                    up.append(a + s[d, i])
                    down.append(a - s[d, i])
                else:
                    up.append(a - s[i, d])
                    down.append(a + s[i, d])
            e = energy_flux(c, w, press, cross, d)
            up.append(c[7] + e)
            down.append(c[7] - e)
            behind.append(up)
            ahead.append(down)
        return c, ahead, behind

    def load_plane(k):
        return [st[plane_at(f, k), :] for f in range(8)]

    def step(k, carry):
        partial, below = carry
        c, ahead, behind = plane_terms(load_plane(k))
        prev = lax.rem(k + planes - 1, planes)
        source = [4.0 * f for f in c]
        source[1] = 4.0 * (c[1] + c[2]) + tidal * c[0]
        source[2] = 4.0 * (c[2] - c[1])
        source[7] = source[7] + tidal * c[1]
        fresh = []
        for f in range(8):
            ov[plane_at(f, prev), :] = partial[f] + ahead[2][f]
            here = 0.5 * bs[plane_at(f, k), :] + source[f]
            here = here + (from_next_x(ahead[0][f]) + from_prev_x(behind[0][f]))
            here = here + (from_next_y(ahead[1][f]) + from_prev_y(behind[1][f]))
            fresh.append(here + below[f])
        return tuple(fresh), tuple(behind[2])

    u = load_plane(planes - 1)
    c, fl = flux_along(u, 2)
    below = tuple(plus(c[f], fl[f]) for f in range(8))
    carry = lax.fori_loop(0, FIRST, step, ((zero,) * 8, below), unroll=2)

    cells = n * ROWS
    shift = jnp.zeros((ROWS, LANES), jnp.int32)
    for k in range(planes):
        shift = jnp.where(pair % 32 == k, shift_ref[k], shift)
    shift = jnp.where(even, shift, jnp.where(shift == 0, 0, cells - shift))
    hop = shift // ROWS
    fine = shift % ROWS
    hop_next = jnp.where(hop == n - 1, 0, hop + 1)

    def locate(hops, target):
        over, rest = hops // inner, hops % inner
        wraps = rest > target
        over = jnp.where(wraps, over + 1, over)
        column = target - rest + jnp.where(wraps, inner, 0)
        return jnp.where(over == outer, 0, over), column

    for copy in edge_copies:
        copy.wait_recv()
    for b in range(inner):
        target = lax.rem(low + b, inner)
        over, column = locate(hop, target)
        over_next, _ = locate(hop_next, target)
        slot = jnp.where(column == low, over, over_next)
        for j in range(4):
            part = pl.ds(j * ROWS, ROWS)
            tile = gath[0, part, :]
            for d in range(1, outer):
                tile = jnp.where(slot == d, gath[d, part, :], tile)
            (relay if b else caught)[b, part, :] = tile
    relay_copies = [relay_copy(d) for d in range(1, inner)]
    for copy in relay_copies:
        copy.start()

    partial, _ = lax.fori_loop(FIRST, planes, step, carry, unroll=2)
    for f in range(8):
        at = plane_at(f, planes - 1)
        ov[at, :] = ov[at, :] + partial[f]

    for s, combine, to_row in ((0, minus, ROWS - 1), (1, plus, 0)):
        halos[s].wait_recv()
        for g in range(planes // ROWS):
            u = [halo_in[s, pl.ds(f * planes + g * ROWS, ROWS), :] for f in range(8)]
            c, fl = flux_along(u, 1)
            for f in range(8):
                at = pl.ds(f * field + g * ROWS * ROWS + to_row, ROWS, stride=ROWS)
                ov[at, :] = ov[at, :] + combine(c[f], fl[f])

    for copy in relay_copies:
        copy.wait_recv()
    near, far = [], []
    for j in range(4):
        part = pl.ds(j * ROWS, ROWS)
        a = b = caught[0, part, :]
        for d in range(1, inner):
            tile = caught[d, part, :]
            a = jnp.where(hop % inner == d, tile, a)
            b = jnp.where(hop_next % inner == d, tile, b)
        near.append(a)
        far.append(b)

    ghost = [None] * 8
    for j in range(4):
        a, b = near[j], far[j]
        for bit in (4, 2, 1):
            ra, rb = pltpu.roll(a, bit, 0), pltpu.roll(b, bit, 0)
            take = (fine // bit) % 2 == 1
            a = jnp.where(take, jnp.where(row < bit, rb, ra), a)
            b = jnp.where(take, rb, b)
        ghost[j] = a
        ghost[j + 4] = pltpu.roll(a, 64, 1)
    sign = jnp.where(even, 1.0, -1.0)
    ghost[0] = jnp.where(lane < 2 * planes, ghost[0], 1.0)
    ghost[2] = ghost[2] + sign * (SHEAR_V * ghost[0])
    c, fl = flux_along(ghost, 0)
    side = []
    for f in range(8):
        e = c[f] if fl[f] is None else c[f] + sign * fl[f]
        side.append(jnp.where(even, pltpu.roll(e, LANES - 1, 1), pltpu.roll(e, 1, 1)))
    for f in range(8):
        side_ref[pl.ds(f * ROWS, ROWS), :] = side[f]

    for copy in halos + edge_copies + relay_copies:
        copy.wait_send()


def finish(planes, inside, side, out_hbm, done, sem):
    lane = lax.broadcasted_iota(jnp.int32, (ROWS, LANES), 1)
    rim = jnp.logical_or(lane == 0, lane == LANES - 1)
    field = planes * ROWS
    copies = []
    for f in range(8):
        edge = side[pl.ds(f * ROWS, ROWS), :]
        for k in range(planes):
            at = pl.ds(f * field + k * ROWS, ROWS)
            add = pltpu.roll(edge, LANES - 1 - 2 * k, 1)
            done[at, :] = inside[at, :] + jnp.where(rim, add, 0.0)
        part = pl.ds(f * field, field)
        copies.append(pltpu.make_async_copy(done.at[part], out_hbm.at[part], sem.at[f]))
        copies[f].start()
    for copy in copies:
        copy.wait()


def on_device(n, state, base, shear_shift):
    shape = state.shape
    planes = shape[1]
    assert shape[0] == 8 and shape[2] == ROWS and shape[3] == LANES and planes == 32
    total = 8 * planes * ROWS
    inner = 1 << ((n.bit_length() - 1) // 2)
    outer = n // inner
    assert outer * inner == n
    inside, side = pl.pallas_call(
        functools.partial(kernel, outer, inner, planes),
        out_shape=(
            pltpu.VMEM((total, LANES), jnp.float32),
            pltpu.VMEM((8 * ROWS, LANES), jnp.float32),
        ),
        in_specs=[
            pl.BlockSpec(memory_space=pltpu.SMEM),
            pl.BlockSpec(memory_space=pltpu.HBM),
            pl.BlockSpec(memory_space=pltpu.HBM),
        ],
        out_specs=[pl.BlockSpec(memory_space=pltpu.VMEM)] * 2,
        scratch_shapes=[
            pltpu.VMEM((total, LANES), jnp.float32),
            pltpu.VMEM((total, LANES), jnp.float32),
            pltpu.VMEM((outer, 4 * ROWS, LANES), jnp.float32),
            pltpu.VMEM((inner, 4 * ROWS, LANES), jnp.float32),
            pltpu.VMEM((inner, 4 * ROWS, LANES), jnp.float32),
            pltpu.VMEM((2, 8 * planes, LANES), jnp.float32),
            pltpu.VMEM((2, 8 * planes, LANES), jnp.float32),
            pltpu.SemaphoreType.DMA((2,)),
            pltpu.SemaphoreType.DMA((2,)),
            pltpu.SemaphoreType.DMA((2,)),
            pltpu.SemaphoreType.DMA((outer,)),
            pltpu.SemaphoreType.DMA((outer,)),
            pltpu.SemaphoreType.DMA((inner,)),
            pltpu.SemaphoreType.DMA((inner,)),
        ],
        compiler_params=pltpu.CompilerParams(
            collective_id=0, has_side_effects=True, vmem_limit_bytes=64 * 1024 * 1024 - 1536 * 1024
        ),
    )(shear_shift, state.reshape(total, LANES), base.reshape(total, LANES))
    out = pl.pallas_call(
        functools.partial(finish, planes),
        out_shape=jax.ShapeDtypeStruct((total, LANES), jnp.float32),
        in_specs=[pl.BlockSpec(memory_space=pltpu.VMEM)] * 2,
        out_specs=pl.BlockSpec(memory_space=pltpu.HBM),
        scratch_shapes=[
            pltpu.VMEM((total, LANES), jnp.float32),
            pltpu.SemaphoreType.DMA((8,)),
        ],
        compiler_params=pltpu.CompilerParams(vmem_limit_bytes=8 * 1024 * 1024),
    )(inside, side)
    return out.reshape(shape)


def solution(mesh):
    return jax.shard_map(
        functools.partial(on_device, mesh.shape["gy"]),
        mesh=mesh,
        in_specs=(P(None, "groups", "gy", None), P(None, "groups", "gy", None), P("groups")),
        out_specs=P(None, "groups", "gy", None),
        check_vma=False,
    )
```

```python
import functools

import jax
import jax.numpy as jnp
from jax import lax
from jax.experimental import pallas as pl
from jax.experimental.pallas import tpu as pltpu
from jax.sharding import PartitionSpec as P

SHEAR_V = 0.75
SCALE = 0.05
LANES = 128
FIRST = 16
ROWS = 8
MESH = pl.DeviceIdType.MESH


def products(u):
    inv = 1.0 / u[0]
    w = [u[1] * inv, u[2] * inv, u[3] * inv]
    b = [u[4], u[5], u[6]]
    c = [SCALE * f for f in u]
    mc, bc = c[1:4], c[4:7]
    kin = mc[0] * w[0] + mc[1] * w[1] + mc[2] * w[2]
    bsq = bc[0] * b[0] + bc[1] * b[1] + bc[2] * b[2]
    press = (2.0 / 3.0) * (c[7] - 0.5 * kin - 0.5 * bsq) + 0.5 * bsq
    cross = w[0] * b[0] + w[1] * b[1] + w[2] * b[2]
    return c, w, b, press, cross


def tensor(c, w, b, i, j):
    return c[1 + i] * w[j] - c[4 + i] * b[j]


def twist(c, w, i, j):
    return w[i] * c[4 + j] - c[4 + i] * w[j]


def energy_flux(c, w, press, cross, d):
    return (c[7] + press) * w[d] - c[4 + d] * cross


def flux_along(u, d):
    c, w, b, press, cross = products(u)
    out = [c[1 + d]]
    for i in range(3):
        t = tensor(c, w, b, i, d)
        out.append(t + press if i == d else t)
    for i in range(3):
        out.append(None if i == d else twist(c, w, d, i))
    out.append(energy_flux(c, w, press, cross, d))
    return c, out


def plus(a, f):
    return a if f is None else a + f


def minus(a, f):
    return a if f is None else a - f


def kernel(
    outer, inner, planes, shift_ref, state_hbm, base_hbm, ov, side_ref,
    st, bs, gath, relay, caught, halo_out, halo_in,
    local_sem, halo_send, halo_recv, edge_send, edge_recv, relay_send, relay_recv,
):
    n = outer * inner
    me = lax.axis_index("gy")
    high, low = me // inner, lax.rem(me, inner)
    field = planes * ROWS
    right = lax.rem(me + 1, n)
    left = lax.rem(me + n - 1, n)

    load_state = pltpu.make_async_copy(state_hbm, st, local_sem.at[0])
    load_state.start()
    load_base = pltpu.make_async_copy(base_hbm, bs, local_sem.at[1])
    load_base.start()

    barrier = pltpu.get_barrier_semaphore()

    across = [lax.rem(me + a * inner, n) for a in range(1, outer)]
    within = [high * inner + lax.rem(low + b, inner) for b in range(1, inner)]
    partners = across + within + [left, right]
    for partner in partners:
        pl.semaphore_signal(
            barrier, inc=1, device_id={"gy": partner}, device_id_type=MESH
        )

    lane = lax.broadcasted_iota(jnp.int32, (ROWS, LANES), 1)
    row = lax.broadcasted_iota(jnp.int32, (ROWS, LANES), 0)
    pair = lane // 2
    even = lane % 2 == 0

    load_state.wait()

    for f in range(8):
        for g in range(planes // ROWS):
            at = f * field + g * ROWS * ROWS
            to = pl.ds(f * planes + g * ROWS, ROWS)
            halo_out[0, to, :] = st[pl.ds(at, ROWS, stride=ROWS), :]
            halo_out[1, to, :] = st[pl.ds(at + ROWS - 1, ROWS, stride=ROWS), :]

    def plane_at(f, k):
        return pl.ds(pl.multiple_of(f * field + k * ROWS, ROWS), ROWS)

    def collect(k, acc):
        out = []
        for j in range(4):
            low = pltpu.roll(st[plane_at(j, k), :], 2 * k + 1, 1)
            high = pltpu.roll(st[plane_at(j + 4, k), :], 2 * k + 1 + 64, 1)
            keep = jnp.where(pair == k, low, acc[j])
            out.append(jnp.where(pair == k + 32, high, keep))
        return tuple(out)

    zero = jnp.zeros((ROWS, LANES), jnp.float32)
    edges = lax.fori_loop(0, planes, collect, (zero,) * 4, unroll=4)
    for j in range(4):
        gath[0, pl.ds(j * ROWS, ROWS), :] = edges[j]

    pl.semaphore_wait(barrier, len(partners))

    def edge_copy(d):
        return pltpu.make_async_remote_copy(
            src_ref=gath.at[0],
            dst_ref=gath.at[d],
            send_sem=edge_send.at[d],
            recv_sem=edge_recv.at[d],
            device_id={"gy": across[d - 1]},
            device_id_type=MESH,
        )

    def relay_copy(d):
        return pltpu.make_async_remote_copy(
            src_ref=relay.at[d],
            dst_ref=caught.at[d],
            send_sem=relay_send.at[d],
            recv_sem=relay_recv.at[d],
            device_id={"gy": within[d - 1]},
            device_id_type=MESH,
        )

    def halo_copy(s, target):
        return pltpu.make_async_remote_copy(
            src_ref=halo_out.at[s],
            dst_ref=halo_in.at[s],
            send_sem=halo_send.at[s],
            recv_sem=halo_recv.at[s],
            device_id={"gy": target},
            device_id_type=MESH,
        )

    edge_copies = [edge_copy(d) for d in range(1, outer)]
    for copy in edge_copies:
        copy.start()
    halos = [halo_copy(0, left), halo_copy(1, right)]
    for copy in halos:
        copy.start()

    load_base.wait()

    tidal = ((lane.astype(jnp.float32) + 0.5) / LANES - 0.5) * 6.0
    first_x, last_x = lane == 0, lane == LANES - 1
    first_y, last_y = row == 0, row == ROWS - 1

    def from_next_x(a):
        return jnp.where(last_x, 0.0, pltpu.roll(a, LANES - 1, 1))

    def from_prev_x(a):
        return jnp.where(first_x, 0.0, pltpu.roll(a, 1, 1))

    def from_next_y(a):
        return jnp.where(last_y, 0.0, pltpu.roll(a, ROWS - 1, 0))

    def from_prev_y(a):
        return jnp.where(first_y, 0.0, pltpu.roll(a, 1, 0))

    def plane_terms(u):
        c, w, b, press, cross = products(u)
        t = {(i, j): tensor(c, w, b, i, j) for i in range(3) for j in range(i, 3)}
        for i in range(3):
            t[i, i] = t[i, i] + press
        s = {(i, j): twist(c, w, i, j) for i in range(3) for j in range(i + 1, 3)}
        ahead, behind = [], []
        for d in range(3):
            fl = [c[1 + d]] + [t[min(i, d), max(i, d)] for i in range(3)]
            up = [c[f] + fl[f] for f in range(4)]
            down = [c[f] - fl[f] for f in range(4)]
            for i in range(3):
                a = c[4 + i]
                if i == d:
                    up.append(a)
                    down.append(a)
                elif d < i:
                    up.append(a + s[d, i])
                    down.append(a - s[d, i])
                else:
                    up.append(a - s[i, d])
                    down.append(a + s[i, d])
            e = energy_flux(c, w, press, cross, d)
            up.append(c[7] + e)
            down.append(c[7] - e)
            behind.append(up)
            ahead.append(down)
        return c, ahead, behind

    def load_plane(k):
        return [st[plane_at(f, k), :] for f in range(8)]

    def step(k, carry):
        partial, below = carry
        c, ahead, behind = plane_terms(load_plane(k))
        prev = lax.rem(k + planes - 1, planes)
        source = [4.0 * f for f in c]
        source[1] = 4.0 * (c[1] + c[2]) + tidal * c[0]
        source[2] = 4.0 * (c[2] - c[1])
        source[7] = source[7] + tidal * c[1]
        fresh = []
        for f in range(8):
            ov[plane_at(f, prev), :] = partial[f] + ahead[2][f]
            here = 0.5 * bs[plane_at(f, k), :] + source[f]
            here = here + (from_next_x(ahead[0][f]) + from_prev_x(behind[0][f]))
            here = here + (from_next_y(ahead[1][f]) + from_prev_y(behind[1][f]))
            fresh.append(here + below[f])
        return tuple(fresh), tuple(behind[2])

    u = load_plane(planes - 1)
    c, fl = flux_along(u, 2)
    below = tuple(plus(c[f], fl[f]) for f in range(8))
    carry = lax.fori_loop(0, FIRST, step, ((zero,) * 8, below), unroll=2)

    cells = n * ROWS
    shift = jnp.zeros((ROWS, LANES), jnp.int32)
    for k in range(planes):
        shift = jnp.where(pair % 32 == k, shift_ref[k], shift)
    shift = jnp.where(even, shift, jnp.where(shift == 0, 0, cells - shift))
    hop = shift // ROWS
    fine = shift % ROWS
    hop_next = jnp.where(hop == n - 1, 0, hop + 1)

    def locate(hops, target):
        over, rest = hops // inner, hops % inner
        wraps = rest > target
        over = jnp.where(wraps, over + 1, over)
        column = target - rest + jnp.where(wraps, inner, 0)
        return jnp.where(over == outer, 0, over), column

    for copy in edge_copies:
        copy.wait_recv()
    for b in range(inner):
        target = lax.rem(low + b, inner)
        over, column = locate(hop, target)
        over_next, _ = locate(hop_next, target)
        slot = jnp.where(column == low, over, over_next)
        for j in range(4):
            part = pl.ds(j * ROWS, ROWS)
            tile = gath[0, part, :]
            for d in range(1, outer):
                tile = jnp.where(slot == d, gath[d, part, :], tile)
            (relay if b else caught)[b, part, :] = tile
    relay_copies = [relay_copy(d) for d in range(1, inner)]
    for copy in relay_copies:
        copy.start()

    partial, _ = lax.fori_loop(FIRST, planes, step, carry, unroll=2)
    for f in range(8):
        at = plane_at(f, planes - 1)
        ov[at, :] = ov[at, :] + partial[f]

    for copy in relay_copies:
        copy.wait_recv()
    near, far = [], []
    for j in range(4):
        part = pl.ds(j * ROWS, ROWS)
        a = b = caught[0, part, :]
        for d in range(1, inner):
            tile = caught[d, part, :]
            a = jnp.where(hop % inner == d, tile, a)
            b = jnp.where(hop_next % inner == d, tile, b)
        near.append(a)
        far.append(b)

    ghost = [None] * 8
    for j in range(4):
        a, b = near[j], far[j]
        for bit in (4, 2, 1):
            ra, rb = pltpu.roll(a, bit, 0), pltpu.roll(b, bit, 0)
            take = (fine // bit) % 2 == 1
            a = jnp.where(take, jnp.where(row < bit, rb, ra), a)
            b = jnp.where(take, rb, b)
        ghost[j] = a
        ghost[j + 4] = pltpu.roll(a, 64, 1)
    sign = jnp.where(even, 1.0, -1.0)
    ghost[0] = jnp.where(lane < 2 * planes, ghost[0], 1.0)
    ghost[2] = ghost[2] + sign * (SHEAR_V * ghost[0])
    c, fl = flux_along(ghost, 0)
    side = []
    for f in range(8):
        e = c[f] if fl[f] is None else c[f] + sign * fl[f]
        side.append(jnp.where(even, pltpu.roll(e, LANES - 1, 1), pltpu.roll(e, 1, 1)))
    for f in range(8):
        side_ref[pl.ds(f * ROWS, ROWS), :] = side[f]

    for s, combine, to_row in ((0, minus, ROWS - 1), (1, plus, 0)):
        halos[s].wait_recv()
        for g in range(planes // ROWS):
            u = [halo_in[s, pl.ds(f * planes + g * ROWS, ROWS), :] for f in range(8)]
            c, fl = flux_along(u, 1)
            for f in range(8):
                at = pl.ds(f * field + g * ROWS * ROWS + to_row, ROWS, stride=ROWS)
                ov[at, :] = ov[at, :] + combine(c[f], fl[f])

    for copy in halos + edge_copies + relay_copies:
        copy.wait_send()


def finish(planes, inside, side, out_hbm, done, sem):
    lane = lax.broadcasted_iota(jnp.int32, (ROWS, LANES), 1)
    rim = jnp.logical_or(lane == 0, lane == LANES - 1)
    field = planes * ROWS
    copies = []
    for f in range(8):
        edge = side[pl.ds(f * ROWS, ROWS), :]
        for k in range(planes):
            at = pl.ds(f * field + k * ROWS, ROWS)
            add = pltpu.roll(edge, LANES - 1 - 2 * k, 1)
            done[at, :] = inside[at, :] + jnp.where(rim, add, 0.0)
        part = pl.ds(f * field, field)
        copies.append(pltpu.make_async_copy(done.at[part], out_hbm.at[part], sem.at[f]))
        copies[f].start()
    for copy in copies:
        copy.wait()


def on_device(n, state, base, shear_shift):
    shape = state.shape
    planes = shape[1]
    assert shape[0] == 8 and shape[2] == ROWS and shape[3] == LANES and planes == 32
    total = 8 * planes * ROWS
    inner = 2
    outer = n // inner
    assert outer * inner == n
    inside, side = pl.pallas_call(
        functools.partial(kernel, outer, inner, planes),
        out_shape=(
            pltpu.VMEM((total, LANES), jnp.float32),
            pltpu.VMEM((8 * ROWS, LANES), jnp.float32),
        ),
        in_specs=[
            pl.BlockSpec(memory_space=pltpu.SMEM),
            pl.BlockSpec(memory_space=pltpu.HBM),
            pl.BlockSpec(memory_space=pltpu.HBM),
        ],
        out_specs=[pl.BlockSpec(memory_space=pltpu.VMEM)] * 2,
        scratch_shapes=[
            pltpu.VMEM((total, LANES), jnp.float32),
            pltpu.VMEM((total, LANES), jnp.float32),
            pltpu.VMEM((outer, 4 * ROWS, LANES), jnp.float32),
            pltpu.VMEM((inner, 4 * ROWS, LANES), jnp.float32),
            pltpu.VMEM((inner, 4 * ROWS, LANES), jnp.float32),
            pltpu.VMEM((2, 8 * planes, LANES), jnp.float32),
            pltpu.VMEM((2, 8 * planes, LANES), jnp.float32),
            pltpu.SemaphoreType.DMA((2,)),
            pltpu.SemaphoreType.DMA((2,)),
            pltpu.SemaphoreType.DMA((2,)),
            pltpu.SemaphoreType.DMA((outer,)),
            pltpu.SemaphoreType.DMA((outer,)),
            pltpu.SemaphoreType.DMA((inner,)),
            pltpu.SemaphoreType.DMA((inner,)),
        ],
        compiler_params=pltpu.CompilerParams(
            collective_id=0, has_side_effects=True, vmem_limit_bytes=64 * 1024 * 1024 - 1536 * 1024
        ),
    )(shear_shift, state.reshape(total, LANES), base.reshape(total, LANES))
    out = pl.pallas_call(
        functools.partial(finish, planes),
        out_shape=jax.ShapeDtypeStruct((total, LANES), jnp.float32),
        in_specs=[pl.BlockSpec(memory_space=pltpu.VMEM)] * 2,
        out_specs=pl.BlockSpec(memory_space=pltpu.HBM),
        scratch_shapes=[
            pltpu.VMEM((total, LANES), jnp.float32),
            pltpu.SemaphoreType.DMA((8,)),
        ],
        compiler_params=pltpu.CompilerParams(vmem_limit_bytes=8 * 1024 * 1024),
    )(inside, side)
    return out.reshape(shape)


def solution(mesh):
    return jax.shard_map(
        functools.partial(on_device, mesh.shape["gy"]),
        mesh=mesh,
        in_specs=(P(None, "groups", "gy", None), P(None, "groups", "gy", None), P("groups")),
        out_specs=P(None, "groups", "gy", None),
        check_vma=False,
    )
```

```python
import functools

import jax
import jax.numpy as jnp
from jax import lax
from jax.experimental import pallas as pl
from jax.experimental.pallas import tpu as pltpu
from jax.sharding import PartitionSpec as P

SHEAR_V = 0.75
SCALE = 0.05
LANES = 128
FIRST = 32
ROWS = 8
MESH = pl.DeviceIdType.MESH


def products(u):
    inv = 1.0 / u[0]
    w = [u[1] * inv, u[2] * inv, u[3] * inv]
    b = [u[4], u[5], u[6]]
    c = [SCALE * f for f in u]
    mc, bc = c[1:4], c[4:7]
    kin = mc[0] * w[0] + mc[1] * w[1] + mc[2] * w[2]
    bsq = bc[0] * b[0] + bc[1] * b[1] + bc[2] * b[2]
    press = (2.0 / 3.0) * (c[7] - 0.5 * kin - 0.5 * bsq) + 0.5 * bsq
    cross = w[0] * b[0] + w[1] * b[1] + w[2] * b[2]
    return c, w, b, press, cross


def tensor(c, w, b, i, j):
    return c[1 + i] * w[j] - c[4 + i] * b[j]


def twist(c, w, i, j):
    return w[i] * c[4 + j] - c[4 + i] * w[j]


def energy_flux(c, w, press, cross, d):
    return (c[7] + press) * w[d] - c[4 + d] * cross


def flux_along(u, d):
    c, w, b, press, cross = products(u)
    out = [c[1 + d]]
    for i in range(3):
        t = tensor(c, w, b, i, d)
        out.append(t + press if i == d else t)
    for i in range(3):
        out.append(None if i == d else twist(c, w, d, i))
    out.append(energy_flux(c, w, press, cross, d))
    return c, out


def plus(a, f):
    return a if f is None else a + f


def minus(a, f):
    return a if f is None else a - f


def kernel(
    outer, inner, planes, shift_ref, state_hbm, base_hbm, ov, side_ref,
    st, bs, gath, relay, caught, halo_out, halo_in,
    local_sem, halo_send, halo_recv, edge_send, edge_recv, relay_send, relay_recv,
):
    n = outer * inner
    me = lax.axis_index("gy")
    high, low = me // inner, lax.rem(me, inner)
    field = planes * ROWS
    right = lax.rem(me + 1, n)
    left = lax.rem(me + n - 1, n)

    load_state = pltpu.make_async_copy(state_hbm, st, local_sem.at[0])
    load_state.start()
    load_base = pltpu.make_async_copy(base_hbm, bs, local_sem.at[1])
    load_base.start()

    barrier = pltpu.get_barrier_semaphore()

    across = [lax.rem(me + a * inner, n) for a in range(1, outer)]
    within = [high * inner + lax.rem(low + b, inner) for b in range(1, inner)]
    partners = across + within + [left, right]
    for partner in partners:
        pl.semaphore_signal(
            barrier, inc=1, device_id={"gy": partner}, device_id_type=MESH
        )

    lane = lax.broadcasted_iota(jnp.int32, (ROWS, LANES), 1)
    row = lax.broadcasted_iota(jnp.int32, (ROWS, LANES), 0)
    pair = lane // 2
    even = lane % 2 == 0

    load_state.wait()

    for f in range(8):
        for g in range(planes // ROWS):
            at = f * field + g * ROWS * ROWS
            to = pl.ds(f * planes + g * ROWS, ROWS)
            halo_out[0, to, :] = st[pl.ds(at, ROWS, stride=ROWS), :]
            halo_out[1, to, :] = st[pl.ds(at + ROWS - 1, ROWS, stride=ROWS), :]

    def plane_at(f, k):
        return pl.ds(pl.multiple_of(f * field + k * ROWS, ROWS), ROWS)

    def collect(k, acc):
        out = []
        for j in range(4):
            low = pltpu.roll(st[plane_at(j, k), :], 2 * k + 1, 1)
            high = pltpu.roll(st[plane_at(j + 4, k), :], 2 * k + 1 + 64, 1)
            keep = jnp.where(pair == k, low, acc[j])
            out.append(jnp.where(pair == k + 32, high, keep))
        return tuple(out)

    zero = jnp.zeros((ROWS, LANES), jnp.float32)
    edges = lax.fori_loop(0, planes, collect, (zero,) * 4, unroll=4)
    for j in range(4):
        gath[0, pl.ds(j * ROWS, ROWS), :] = edges[j]

    pl.semaphore_wait(barrier, len(partners))

    def edge_copy(d):
        return pltpu.make_async_remote_copy(
            src_ref=gath.at[0],
            dst_ref=gath.at[d],
            send_sem=edge_send.at[d],
            recv_sem=edge_recv.at[d],
            device_id={"gy": across[d - 1]},
            device_id_type=MESH,
        )

    def relay_copy(d):
        return pltpu.make_async_remote_copy(
            src_ref=relay.at[d],
            dst_ref=caught.at[d],
            send_sem=relay_send.at[d],
            recv_sem=relay_recv.at[d],
            device_id={"gy": within[d - 1]},
            device_id_type=MESH,
        )

    def halo_copy(s, target):
        return pltpu.make_async_remote_copy(
            src_ref=halo_out.at[s],
            dst_ref=halo_in.at[s],
            send_sem=halo_send.at[s],
            recv_sem=halo_recv.at[s],
            device_id={"gy": target},
            device_id_type=MESH,
        )

    edge_copies = [edge_copy(d) for d in range(1, outer)]
    for copy in edge_copies:
        copy.start()
    halos = [halo_copy(0, left), halo_copy(1, right)]
    for copy in halos:
        copy.start()

    load_base.wait()

    tidal = ((lane.astype(jnp.float32) + 0.5) / LANES - 0.5) * 6.0
    first_x, last_x = lane == 0, lane == LANES - 1
    first_y, last_y = row == 0, row == ROWS - 1

    def from_next_x(a):
        return jnp.where(last_x, 0.0, pltpu.roll(a, LANES - 1, 1))

    def from_prev_x(a):
        return jnp.where(first_x, 0.0, pltpu.roll(a, 1, 1))

    def from_next_y(a):
        return jnp.where(last_y, 0.0, pltpu.roll(a, ROWS - 1, 0))

    def from_prev_y(a):
        return jnp.where(first_y, 0.0, pltpu.roll(a, 1, 0))

    def plane_terms(u):
        c, w, b, press, cross = products(u)
        t = {(i, j): tensor(c, w, b, i, j) for i in range(3) for j in range(i, 3)}
        for i in range(3):
            t[i, i] = t[i, i] + press
        s = {(i, j): twist(c, w, i, j) for i in range(3) for j in range(i + 1, 3)}
        ahead, behind = [], []
        for d in range(3):
            fl = [c[1 + d]] + [t[min(i, d), max(i, d)] for i in range(3)]
            up = [c[f] + fl[f] for f in range(4)]
            down = [c[f] - fl[f] for f in range(4)]
            for i in range(3):
                a = c[4 + i]
                if i == d:
                    up.append(a)
                    down.append(a)
                elif d < i:
                    up.append(a + s[d, i])
                    down.append(a - s[d, i])
                else:
                    up.append(a - s[i, d])
                    down.append(a + s[i, d])
            e = energy_flux(c, w, press, cross, d)
            up.append(c[7] + e)
            down.append(c[7] - e)
            behind.append(up)
            ahead.append(down)
        return c, ahead, behind

    def load_plane(k):
        return [st[plane_at(f, k), :] for f in range(8)]

    def step(k, carry):
        partial, below = carry
        c, ahead, behind = plane_terms(load_plane(k))
        prev = lax.rem(k + planes - 1, planes)
        source = [4.0 * f for f in c]
        source[1] = 4.0 * (c[1] + c[2]) + tidal * c[0]
        source[2] = 4.0 * (c[2] - c[1])
        source[7] = source[7] + tidal * c[1]
        fresh = []
        for f in range(8):
            ov[plane_at(f, prev), :] = partial[f] + ahead[2][f]
            here = 0.5 * bs[plane_at(f, k), :] + source[f]
            here = here + (from_next_x(ahead[0][f]) + from_prev_x(behind[0][f]))
            here = here + (from_next_y(ahead[1][f]) + from_prev_y(behind[1][f]))
            fresh.append(here + below[f])
        return tuple(fresh), tuple(behind[2])

    u = load_plane(planes - 1)
    c, fl = flux_along(u, 2)
    below = tuple(plus(c[f], fl[f]) for f in range(8))
    carry = lax.fori_loop(0, FIRST, step, ((zero,) * 8, below), unroll=2)

    cells = n * ROWS
    shift = jnp.zeros((ROWS, LANES), jnp.int32)
    for k in range(planes):
        shift = jnp.where(pair % 32 == k, shift_ref[k], shift)
    shift = jnp.where(even, shift, jnp.where(shift == 0, 0, cells - shift))
    hop = shift // ROWS
    fine = shift % ROWS
    hop_next = jnp.where(hop == n - 1, 0, hop + 1)

    def locate(hops, target):
        over, rest = hops // inner, hops % inner
        wraps = rest > target
        over = jnp.where(wraps, over + 1, over)
        column = target - rest + jnp.where(wraps, inner, 0)
        return jnp.where(over == outer, 0, over), column

    for copy in edge_copies:
        copy.wait_recv()
    for b in range(inner):
        target = lax.rem(low + b, inner)
        over, column = locate(hop, target)
        over_next, _ = locate(hop_next, target)
        slot = jnp.where(column == low, over, over_next)
        for j in range(4):
            part = pl.ds(j * ROWS, ROWS)
            tile = gath[0, part, :]
            for d in range(1, outer):
                tile = jnp.where(slot == d, gath[d, part, :], tile)
            (relay if b else caught)[b, part, :] = tile
    relay_copies = [relay_copy(d) for d in range(1, inner)]
    for copy in relay_copies:
        copy.start()

    partial, _ = lax.fori_loop(FIRST, planes, step, carry, unroll=2)
    for f in range(8):
        at = plane_at(f, planes - 1)
        ov[at, :] = ov[at, :] + partial[f]

    for copy in relay_copies:
        copy.wait_recv()
    near, far = [], []
    for j in range(4):
        part = pl.ds(j * ROWS, ROWS)
        a = b = caught[0, part, :]
        for d in range(1, inner):
            tile = caught[d, part, :]
            a = jnp.where(hop % inner == d, tile, a)
            b = jnp.where(hop_next % inner == d, tile, b)
        near.append(a)
        far.append(b)

    ghost = [None] * 8
    for j in range(4):
        a, b = near[j], far[j]
        for bit in (4, 2, 1):
            ra, rb = pltpu.roll(a, bit, 0), pltpu.roll(b, bit, 0)
            take = (fine // bit) % 2 == 1
            a = jnp.where(take, jnp.where(row < bit, rb, ra), a)
            b = jnp.where(take, rb, b)
        ghost[j] = a
        ghost[j + 4] = pltpu.roll(a, 64, 1)
    sign = jnp.where(even, 1.0, -1.0)
    ghost[0] = jnp.where(lane < 2 * planes, ghost[0], 1.0)
    ghost[2] = ghost[2] + sign * (SHEAR_V * ghost[0])
    c, fl = flux_along(ghost, 0)
    side = []
    for f in range(8):
        e = c[f] if fl[f] is None else c[f] + sign * fl[f]
        side.append(jnp.where(even, pltpu.roll(e, LANES - 1, 1), pltpu.roll(e, 1, 1)))
    for f in range(8):
        side_ref[pl.ds(f * ROWS, ROWS), :] = side[f]

    for s, combine, to_row in ((0, minus, ROWS - 1), (1, plus, 0)):
        halos[s].wait_recv()
        for g in range(planes // ROWS):
            u = [halo_in[s, pl.ds(f * planes + g * ROWS, ROWS), :] for f in range(8)]
            c, fl = flux_along(u, 1)
            for f in range(8):
                at = pl.ds(f * field + g * ROWS * ROWS + to_row, ROWS, stride=ROWS)
                ov[at, :] = ov[at, :] + combine(c[f], fl[f])

    for copy in halos + edge_copies + relay_copies:
        copy.wait_send()


def finish(planes, inside, side, out_hbm, done, sem):
    lane = lax.broadcasted_iota(jnp.int32, (ROWS, LANES), 1)
    rim = jnp.logical_or(lane == 0, lane == LANES - 1)
    field = planes * ROWS
    copies = []
    for f in range(8):
        edge = side[pl.ds(f * ROWS, ROWS), :]
        for k in range(planes):
            at = pl.ds(f * field + k * ROWS, ROWS)
            add = pltpu.roll(edge, LANES - 1 - 2 * k, 1)
            done[at, :] = inside[at, :] + jnp.where(rim, add, 0.0)
        part = pl.ds(f * field, field)
        copies.append(pltpu.make_async_copy(done.at[part], out_hbm.at[part], sem.at[f]))
        copies[f].start()
    for copy in copies:
        copy.wait()


def on_device(n, state, base, shear_shift):
    shape = state.shape
    planes = shape[1]
    assert shape[0] == 8 and shape[2] == ROWS and shape[3] == LANES and planes == 32
    total = 8 * planes * ROWS
    inner = 2
    outer = n // inner
    assert outer * inner == n
    inside, side = pl.pallas_call(
        functools.partial(kernel, outer, inner, planes),
        out_shape=(
            pltpu.VMEM((total, LANES), jnp.float32),
            pltpu.VMEM((8 * ROWS, LANES), jnp.float32),
        ),
        in_specs=[
            pl.BlockSpec(memory_space=pltpu.SMEM),
            pl.BlockSpec(memory_space=pltpu.HBM),
            pl.BlockSpec(memory_space=pltpu.HBM),
        ],
        out_specs=[pl.BlockSpec(memory_space=pltpu.VMEM)] * 2,
        scratch_shapes=[
            pltpu.VMEM((total, LANES), jnp.float32),
            pltpu.VMEM((total, LANES), jnp.float32),
            pltpu.VMEM((outer, 4 * ROWS, LANES), jnp.float32),
            pltpu.VMEM((inner, 4 * ROWS, LANES), jnp.float32),
            pltpu.VMEM((inner, 4 * ROWS, LANES), jnp.float32),
            pltpu.VMEM((2, 8 * planes, LANES), jnp.float32),
            pltpu.VMEM((2, 8 * planes, LANES), jnp.float32),
            pltpu.SemaphoreType.DMA((2,)),
            pltpu.SemaphoreType.DMA((2,)),
            pltpu.SemaphoreType.DMA((2,)),
            pltpu.SemaphoreType.DMA((outer,)),
            pltpu.SemaphoreType.DMA((outer,)),
            pltpu.SemaphoreType.DMA((inner,)),
            pltpu.SemaphoreType.DMA((inner,)),
        ],
        compiler_params=pltpu.CompilerParams(
            collective_id=0, has_side_effects=True, vmem_limit_bytes=64 * 1024 * 1024 - 1536 * 1024
        ),
    )(shear_shift, state.reshape(total, LANES), base.reshape(total, LANES))
    out = pl.pallas_call(
        functools.partial(finish, planes),
        out_shape=jax.ShapeDtypeStruct((total, LANES), jnp.float32),
        in_specs=[pl.BlockSpec(memory_space=pltpu.VMEM)] * 2,
        out_specs=pl.BlockSpec(memory_space=pltpu.HBM),
        scratch_shapes=[
            pltpu.VMEM((total, LANES), jnp.float32),
            pltpu.SemaphoreType.DMA((8,)),
        ],
        compiler_params=pltpu.CompilerParams(vmem_limit_bytes=8 * 1024 * 1024),
    )(inside, side)
    return out.reshape(shape)


def solution(mesh):
    return jax.shard_map(
        functools.partial(on_device, mesh.shape["gy"]),
        mesh=mesh,
        in_specs=(P(None, "groups", "gy", None), P(None, "groups", "gy", None), P("groups")),
        out_specs=P(None, "groups", "gy", None),
        check_vma=False,
    )
```
